32 devices in a mesh: groups: 2 (over x), tensor: 4 (over y, core), replica: 4 (over z).
Axes of the slice: x: 2, y: 2, z: 4, core: 2. Of those that a mesh axis runs over, the one named last changes fastest.
Arguments:
- normed_hidden_input: bfloat16 [2048, 8192], P(('groups', 'replica'), 'tensor'), parts along dimension 0, may hold values from -6 to 6
- attention_heads_context: bfloat16 [2048, 8192], P(('groups', 'replica'), 'tensor'), parts along dimension 0, may hold values from -6 to 6
- query_weight_matrix: bfloat16 [8192, 8192], P('tensor', 'replica'), may hold values from -0.0625 to 0.0625
- keyval_weight_matrix: bfloat16 [8192, 2048], P('tensor', 'replica'), may hold values from -0.0625 to 0.0625
- output_weight_matrix: bfloat16 [8192, 8192], P('tensor', 'replica'), may hold values from -0.0625 to 0.0625
- down_qkv: bfloat16 [128, 8192, 192], P(('groups', 'replica'), 'tensor'), parts along dimension 0, may hold values from -0.0625 to 0.0625
- down_out: bfloat16 [128, 8192, 64], P(('groups', 'replica'), 'tensor'), parts along dimension 0, may hold values from -0.0625 to 0.0625
- up_query: bfloat16 [128, 64, 8192], P(('groups', 'tensor'), None, 'replica'), parts along dimension 0, may hold values from -0.75 to 0.75
- up_keyval: bfloat16 [128, 64, 2048], P(('groups', 'tensor'), None, 'replica'), parts along dimension 0, may hold values from -0.75 to 0.75
- up_output: bfloat16 [128, 64, 8192], P(('groups', 'tensor'), None, 'replica'), parts along dimension 0, may hold values from -0.75 to 0.75
- seg_lengths: int32 [32], P('groups'), parts along dimension 0, may hold values from 1 to 256, 1024 in all
- seg_adapter: int32 [32], P('groups'), parts along dimension 0, may hold values from 0 to 63
- adapter_rank: int32 [128], P('groups'), parts along dimension 0, may hold values from 16 to 64
Outputs:
- query: bfloat16 [2048, 8192], P(('groups', 'tensor'), 'replica'), parts along dimension 0
- keyval: bfloat16 [2048, 2048], P(('groups', 'tensor'), 'replica'), parts along dimension 0
- adapted_output_matrix: bfloat16 [2048, 8192], P(('groups', 'tensor'), 'replica'), parts along dimension 0
The draws below stay inside these ranges and needn't reach their ends.
There are 2 independent parts, one for each index of `groups`. The reference program is written for one: setup_inputs(seed, part) draws one part's arguments, and reference() takes and returns one part's arrays. A program takes and returns all parts, laid end to end along the dimension named above; an argument that names none is the same for every part. Nothing has to cross between parts.
Inputs may be any that keep to these rules, and one draw needn't show every extreme that they name: `seg_lengths`: 16 request lengths that sum to 1024; the longest is exactly 256. `seg_adapter`: an adapter index below 64 for each request. `adapter_rank`: each adapter's rank, at most 64.
All inputs are finite; a program needn't handle non-finite values.
Results may differ from the reference program's by a relative error of at most 0.0038.
Values may be sent and summed in bfloat16 or wider, within the bound.
A program may use at most 192 MiB of HBM per device.

```python
import math
import jax
import jax.numpy as jnp
import numpy as np
from jax import lax

D = 8192
QD = 8192
KVD = 1024
R = 64
REQUEST_SEGMENTS = 16
ADP = 64
TOKENS = 1024
MOST = 256


def place_ends(entries, key, low, largest):
    dims = entries.shape
    spot = [jax.random.randint(jax.random.fold_in(key, axis), (), 0, dims[axis]) for axis in range(len(dims))]
    entries = entries.at[tuple(spot)].set(low)
    longest = dims.index(max(dims))
    spot[longest] = (spot[longest] + 1) % dims[longest]
    return entries.at[tuple(spot)].set(largest)


def shard_levels(key, dims, pieces, low, high):
    loudness, own = 1.0, jax.random.fold_in(key, 6)
    for position, parts in pieces:
        draws = jnp.exp(jax.random.uniform(jax.random.fold_in(own, position), (parts,), jnp.float32, low / len(pieces), high / len(pieces)))
        loudness = loudness * jnp.repeat(draws, dims[position] // parts).reshape([-1 if axis == position else 1 for axis in range(len(dims))])
    return loudness


def cumulative_ranks(count, slope):
    portions = [(1 << 20) // math.isqrt(grade ** slope) + 1 for grade in range(1, count + 1)]
    width = 1 + sum(portions) // (1 << 30)
    return np.cumsum(np.array([max(1, weight // width) for weight in portions]))


def skewed_ids(own_key, shape, number_of, skew):
    listing = cumulative_ranks(number_of, skew)
    ticket = jax.random.randint(jax.random.fold_in(own_key, 1), shape, 0, int(listing[number_of - 1]))
    grade = jnp.searchsorted(jnp.asarray(listing, jnp.int32), ticket, side="right")
    return jax.random.permutation(jax.random.fold_in(own_key, 2), number_of)[grade].astype(jnp.int32)


def profile(number_of, total, reach, slope):
    loads = [(1 << 20) // math.isqrt(rank ** slope) + 1 for rank in range(2, number_of + 1)]
    spare, given = total - reach - (number_of - 1), [1] * (number_of - 1)
    while spare > 0:
        movable = [i for i in range(number_of - 1) if given[i] < reach]
        pool, remaining = sum([loads[i] for i in movable]), spare
        for i in movable:
            addition = min(reach - given[i], max(1, remaining * loads[i] // pool), spare)
            given[i] = given[i] + addition
            spare = spare - addition
    return np.array([reach] + given)


def ragged_sizes(own_key, amount, total, most, lean):
    if amount == 2:
        one = jax.random.randint(own_key, (), max(1, total - most), min(most, total - 1) + 1)
        return jnp.stack([one, total - one])
    lengths = jnp.asarray(profile(amount, total, most, lean), jnp.int32)
    twos = (amount - 1) // 2
    donor, receiver = lengths[1:1 + 2 * twos:2], lengths[2:2 + 2 * twos:2]
    slack = jnp.minimum(donor - 1, most - receiver)
    shifted = jax.random.randint(jax.random.fold_in(own_key, 1), (twos,), 0, 1 << 20) % (slack + 1)
    lengths = lengths.at[1:1 + 2 * twos:2].set(donor - shifted).at[2:2 + 2 * twos:2].set(receiver + shifted)
    return lengths[jax.random.permutation(jax.random.fold_in(own_key, 2), amount)]


def bell_draw(own_key, extent, spread, limit, pieces=(), kind=jnp.bfloat16):
    result = jax.random.normal(own_key, extent, jnp.float32) * spread
    if len(pieces) > 0:
        result = shard_levels(own_key, extent, pieces, -0.22, 0.18) * result
    return jnp.clip(result, min=-limit, max=limit).astype(kind)


def setup_inputs(seed: int = 0, part: int = 0) -> dict:
    keys = jax.random.split(jax.random.key(seed), 14)
    part_splits = jax.random.split(jax.random.fold_in(keys[13], part), 14)
    return {
        "normed_hidden_input": bell_draw(part_splits[0], (TOKENS, D), 1.0, 6.0, ((0, 4), (1, 4))),
        "attention_heads_context": bell_draw(part_splits[1], (TOKENS, QD), 1.0, 6.0, ((0, 4), (1, 4))),
        "query_weight_matrix": bell_draw(keys[2], (D, QD), D ** -0.5, 0.0625, ((0, 4), (1, 4))),
        "keyval_weight_matrix": bell_draw(keys[3], (D, 2 * KVD), D ** -0.5, 0.0625, ((0, 4), (1, 4))),
        "output_weight_matrix": bell_draw(keys[4], (QD, D), QD ** -0.5, 0.0625, ((0, 4), (1, 4))),
        "down_qkv": bell_draw(part_splits[5], (ADP, D, 3 * R), D ** -0.5, 0.0625, ((0, 4), (1, 4))),
        "down_out": bell_draw(part_splits[6], (ADP, QD, R), QD ** -0.5, 0.0625, ((0, 4), (1, 4))),
        "up_query": bell_draw(part_splits[7], (ADP, R, QD), R ** -0.5, 0.75, ((0, 4), (2, 4))),
        "up_keyval": bell_draw(part_splits[8], (ADP, R, 2 * KVD), R ** -0.5, 0.75, ((0, 4), (2, 4))),
        "up_output": bell_draw(part_splits[9], (ADP, R, D), R ** -0.5, 0.75, ((0, 4), (2, 4))),
        "seg_lengths": ragged_sizes(part_splits[10], REQUEST_SEGMENTS, TOKENS, MOST, 2).astype(jnp.int32),
        "seg_adapter": place_ends(skewed_ids(part_splits[11], (REQUEST_SEGMENTS,), ADP, 2), jax.random.fold_in(part_splits[11], 3), 0, ADP - 1).astype(jnp.int32),
        "adapter_rank": place_ends(jax.random.randint(part_splits[12], (ADP,), R // 4, R + 1), jax.random.fold_in(part_splits[12], 1), R // 4, R).astype(jnp.int32),
    }


def reference(normed_hidden_input, attention_heads_context, query_weight_matrix, keyval_weight_matrix, output_weight_matrix, down_qkv, down_out, up_query, up_keyval, up_output, seg_lengths, seg_adapter, adapter_rank):
    seg_ends = jnp.cumsum(seg_lengths).astype(jnp.int32)
    positions = jnp.arange(TOKENS, dtype=jnp.int32)
    seg_index = jnp.sum((positions[:, None] >= seg_ends[None, :]).astype(jnp.int32), axis=1)
    adapter = seg_adapter[seg_index]
    rank = adapter_rank[adapter]
    columns = jnp.arange(R, dtype=jnp.int32)
    keep = jnp.where(columns[None, :] < rank[:, None], (0.5 * R) / rank.astype(jnp.float32)[:, None], 0.0)

    def down_step(total, segment):
        chosen = seg_adapter[segment]
        inside = (seg_index == segment)[:, None]
        low_qkv = jnp.dot(normed_hidden_input, down_qkv[chosen], preferred_element_type=jnp.float32)
        low_out = jnp.dot(attention_heads_context, down_out[chosen], preferred_element_type=jnp.float32)
        return total + jnp.where(inside, jnp.concatenate([low_qkv, low_out], axis=1), 0.0), None

    low_full, unused_value = lax.scan(down_step, jnp.zeros((TOKENS, 4 * R), jnp.float32), jnp.arange(REQUEST_SEGMENTS, dtype=jnp.int32))
    rank_act = (low_full * jnp.tile(keep, (1, 4))).astype(jnp.bfloat16)
    rank_query = rank_act[:, :R]
    rank_key = rank_act[:, R:2 * R]
    rank_value = rank_act[:, 2 * R:3 * R]
    rank_out = rank_act[:, 3 * R:]

    def upward_product_step(totals, segment):
        chosen = seg_adapter[segment]
        inside = (seg_index == segment)[:, None]
        table = up_keyval[chosen]
        term_query = jnp.dot(rank_query, up_query[chosen], preferred_element_type=jnp.float32)
        term_key = jnp.dot(rank_key, table[:, :KVD], preferred_element_type=jnp.float32)
        term_value = jnp.dot(rank_value, table[:, KVD:], preferred_element_type=jnp.float32)
        term_out = jnp.dot(rank_out, up_output[chosen], preferred_element_type=jnp.float32)
        term_keyval = jnp.concatenate([term_key, term_value], axis=1)
        return (totals[0] + jnp.where(inside, term_query, 0.0), totals[1] + jnp.where(inside, term_keyval, 0.0), totals[2] + jnp.where(inside, term_out, 0.0)), None

    initial_partial_sums = (jnp.zeros((TOKENS, QD), jnp.float32), jnp.zeros((TOKENS, 2 * KVD), jnp.float32), jnp.zeros((TOKENS, D), jnp.float32))
    adapter_partial_sums, unused_value = lax.scan(upward_product_step, initial_partial_sums, jnp.arange(REQUEST_SEGMENTS, dtype=jnp.int32))
    query = (jnp.dot(normed_hidden_input, query_weight_matrix, preferred_element_type=jnp.float32) + adapter_partial_sums[0]).astype(jnp.bfloat16)
    keyval = (jnp.dot(normed_hidden_input, keyval_weight_matrix, preferred_element_type=jnp.float32) + adapter_partial_sums[1]).astype(jnp.bfloat16)
    adapted_output_matrix = (jnp.dot(attention_heads_context, output_weight_matrix, preferred_element_type=jnp.float32) + adapter_partial_sums[2]).astype(jnp.bfloat16)
    return (query, keyval, adapted_output_matrix)
```

```python
import functools

import jax
import jax.numpy as jnp
from jax import lax
from jax.experimental import pallas as pl
from jax.experimental.pallas import tpu as pltpu
from jax.sharding import PartitionSpec as P

KVD = 1024


def low_kernel(first_ref, adapter_ref, x_ref, table_ref, low_ref):
    a = pl.program_id(0)

    @pl.when(a == 0)
    def _():
        low_ref[...] = jnp.zeros_like(low_ref)

    term = jnp.dot(x_ref[...], table_ref[0], preferred_element_type=jnp.float32)
    low_ref[...] += jnp.where(adapter_ref[...] == first_ref[0] + a, term, 0.0)


def low_rows(x, table, adapter, first):
    rows, depth = x.shape
    count, _, width = table.shape
    return pl.pallas_call(
        low_kernel,
        grid_spec=pltpu.PrefetchScalarGridSpec(
            num_scalar_prefetch=1,
            grid=(count,),
            in_specs=[
                pl.BlockSpec((rows, 1), lambda a, s: (0, 0)),
                pl.BlockSpec((rows, depth), lambda a, s: (0, 0)),
                pl.BlockSpec((1, depth, width), lambda a, s: (a, 0, 0)),
            ],
            out_specs=pl.BlockSpec((rows, width), lambda a, s: (0, 0)),
        ),
        out_shape=jax.ShapeDtypeStruct((rows, width), jnp.float32),
        compiler_params=pltpu.CompilerParams(vmem_limit_bytes=40 * 2**20),
        cost_estimate=pl.CostEstimate(
            flops=2 * rows * depth * width * count,
            bytes_accessed=2 * (rows * depth + count * depth * width),
            transcendentals=0,
        ),
    )(first, adapter[:, None], x, table)


def token_tables(seg_lengths, seg_adapter, adapter_rank, total, rank_width):
    seg_ends = jnp.cumsum(seg_lengths)
    positions = jnp.arange(total, dtype=jnp.int32)
    seg_index = jnp.sum((positions[:, None] >= seg_ends[None, :]).astype(jnp.int32), axis=1)
    seg_hot = seg_index[:, None] == jnp.arange(seg_lengths.shape[0], dtype=jnp.int32)[None, :]
    adapter = jnp.sum(jnp.where(seg_hot, seg_adapter[None, :], 0), axis=1)
    adapter_hot = adapter[:, None] == jnp.arange(adapter_rank.shape[0], dtype=jnp.int32)[None, :]
    rank = jnp.sum(jnp.where(adapter_hot, adapter_rank[None, :], 0), axis=1)
    columns = jnp.arange(rank_width, dtype=jnp.int32)
    keep = jnp.where(
        columns[None, :] < rank[:, None], 0.5 * rank_width / rank.astype(jnp.float32)[:, None], 0.0
    )
    return adapter, keep


def shards(h, c, wq, wkv, wo, dqkv, dout, upq, upkv, upo, seg_lengths, seg_adapter, adapter_rank):
    hidden = lax.all_gather(h, "replica", axis=0, tiled=True)
    context = lax.all_gather(c, "replica", axis=0, tiled=True)
    total = hidden.shape[0]
    r = upq.shape[1]
    adapter, keep = token_tables(seg_lengths, seg_adapter, adapter_rank, total, r)
    first_down = (lax.axis_index("replica") * dqkv.shape[0]).astype(jnp.int32)[None]
    up_count = upq.shape[0]
    owner = lax.axis_index("tensor") * up_count + jnp.arange(up_count * r, dtype=jnp.int32) // r
    mine = adapter[:, None] == owner[None, :]

    def part(x, w, ranks, up):
        spread = jnp.where(mine, jnp.tile(ranks, (1, up_count)), jnp.bfloat16(0))
        up2 = up.reshape(up_count * r, up.shape[2])
        return (
            jnp.dot(x, w, preferred_element_type=jnp.float32)
            + jnp.dot(spread, up2, preferred_element_type=jnp.float32)
        ).astype(jnp.bfloat16)

    def reduce_rows(x):
        return lax.psum_scatter(x, "tensor", scatter_dimension=0, tiled=True)

    low_qkv = lax.psum(low_rows(hidden, dqkv, adapter, first_down), ("tensor", "replica"))
    act = (low_qkv * jnp.tile(keep, (1, 3))).astype(jnp.bfloat16)
    kv_width = upkv.shape[2]
    kv_start = lax.axis_index("replica") * kv_width
    rank_kv = jnp.where(kv_start >= KVD, act[:, 2 * r :], act[:, r : 2 * r])
    query = reduce_rows(part(hidden, wq, act[:, :r], upq))
    keyval = reduce_rows(part(hidden, wkv, rank_kv, upkv))
    low_out = lax.psum(low_rows(context, dout, adapter, first_down), ("tensor", "replica"))
    act_out = (low_out * keep).astype(jnp.bfloat16)
    out = reduce_rows(part(context, wo, act_out, upo))
    return query, keyval, out


def solution(mesh):
    in_specs = (
        P(("groups", "replica"), "tensor"),
        P(("groups", "replica"), "tensor"),
        P("tensor", "replica"),
        P("tensor", "replica"),
        P("tensor", "replica"),
        P(("groups", "replica"), "tensor", None),
        P(("groups", "replica"), "tensor", None),
        P(("groups", "tensor"), None, "replica"),
        P(("groups", "tensor"), None, "replica"),
        P(("groups", "tensor"), None, "replica"),
        P("groups"),
        P("groups"),
        P("groups"),
    )
    out_specs = (P(("groups", "tensor"), "replica"),) * 3
    return jax.shard_map(shards, mesh=mesh, in_specs=in_specs, out_specs=out_specs, check_vma=False)
```

```python
import functools

import jax
import jax.numpy as jnp
from jax import lax
from jax.experimental import pallas as pl
from jax.experimental.pallas import tpu as pltpu
from jax.sharding import PartitionSpec as P

KVD = 1024
PIECES = 1
OUT_CHUNKS = 2
TRANSPOSED = (((1,), (1,)), ((), ()))


def low_kernel(first_ref, adapter_ref, x_ref, table_ref, low_ref):
    step = pl.program_id(0)
    together, width, depth = table_ref.shape

    @pl.when(step == 0)
    def _():
        low_ref[...] = jnp.zeros_like(low_ref)

    term = lax.dot_general(
        x_ref[...],
        table_ref[...].reshape(together * width, depth),
        TRANSPOSED,
        preferred_element_type=jnp.float32,
    )
    adapter = adapter_ref[...]
    low = low_ref[...]
    for i in range(together):
        chosen = adapter == first_ref[0] + step * together + i
        low = low + jnp.where(chosen, term[:, i * width : (i + 1) * width], 0.0)
    low_ref[...] = low


def low_rows(x, table, adapter, first):
    rows, depth = x.shape
    count, width, _ = table.shape
    together = min(count, max(1, 256 // width))
    return pl.pallas_call(
        low_kernel,
        grid_spec=pltpu.PrefetchScalarGridSpec(
            num_scalar_prefetch=1,
            grid=(count // together,),
            in_specs=[
                pl.BlockSpec((rows, 1), lambda a, s: (0, 0)),
                pl.BlockSpec((rows, depth), lambda a, s: (0, 0)),
                pl.BlockSpec((together, width, depth), lambda a, s: (a, 0, 0)),
            ],
            out_specs=pl.BlockSpec((rows, width), lambda a, s: (0, 0)),
        ),
        out_shape=jax.ShapeDtypeStruct((rows, width), jnp.float32),
        compiler_params=pltpu.CompilerParams(vmem_limit_bytes=56 * 2**20),
        cost_estimate=pl.CostEstimate(
            flops=2 * rows * depth * width * count,
            bytes_accessed=2 * (rows * depth + count * depth * width),
            transcendentals=0,
        ),
    )(first, adapter, x, table)


def act_kernel(
    nt, nz, low_ref, keep_ref, act_ref, near, pair, cross, mine, far,
    s1, r1, s2, r2, s3, r3, s4, r4, s5, r5,
):
    t, z = lax.axis_index("tensor"), lax.axis_index("replica")
    ny = nt // 2
    y, core = t // 2, lax.rem(t, 2)
    rows, width = mine.shape
    partner = {"tensor": t + 1 - 2 * core}
    columns = [{"tensor": 2 * lax.rem(y + d, ny) + core} for d in range(1, ny)]
    planes = [{"replica": lax.rem(z + d, nz)} for d in range(1, nz)]
    barrier = pltpu.get_barrier_semaphore()
    for peer in [partner] + columns + planes:
        pl.semaphore_signal(barrier, inc=1, device_id=peer)
    pl.semaphore_wait(barrier, 1 + len(columns) + len(planes))

    def block(index):
        return pl.ds(pl.multiple_of(index * rows, rows), rows)

    def send_all(jobs, sends, recvs):
        copies = [
            pltpu.make_async_remote_copy(src, dst, sends.at[i], recvs.at[i], device_id=peer)
            for i, (src, dst, peer) in enumerate(jobs)
        ]
        for copy in copies:
            copy.start()
        for copy in copies:
            copy.wait()

    send_all(
        [(low_ref.at[block(2 * j + 1 - core)], near.at[j], partner) for j in range(ny)], s1, r1
    )
    for j in range(ny):
        pair[j] = low_ref[block(2 * j + core), :] + near[j]
    send_all(
        [
            (pair.at[lax.rem(y + d, ny)], cross.at[d - 1], columns[d - 1])
            for d in range(1, ny)
        ],
        s2,
        r2,
    )
    total = pair[y]
    for d in range(1, ny):
        total = total + cross[d - 1]
    keep = keep_ref[block(t), :]
    own = (total * jnp.concatenate([keep] * (width // keep.shape[1]), axis=1)).astype(jnp.bfloat16)
    mine[...] = own
    send_all([(mine, far.at[i], peer) for i, peer in enumerate(planes)], s3, r3)
    total = own.astype(jnp.float32)
    for d in range(1, nz):
        total = total + far[d - 1].astype(jnp.float32)
    act_ref[block(t), :] = total.astype(jnp.bfloat16)
    send_all([(act_ref.at[block(t)], act_ref.at[block(t)], peer) for peer in columns], s4, r4)
    send_all(
        [
            (act_ref.at[block(2 * j + core)], act_ref.at[block(2 * j + core)], partner)
            for j in range(ny)
        ],
        s5,
        r5,
    )


def rank_rows(low, keep, nt, nz, collective_id):
    total, width = low.shape
    rows = total // nt
    vmem = pl.BlockSpec(memory_space=pltpu.VMEM)
    ny = nt // 2
    pairs, across, planes = (pltpu.SemaphoreType.DMA((n,)) for n in (ny, ny - 1, nz - 1))
    return pl.pallas_call(
        functools.partial(act_kernel, nt, nz),
        in_specs=[vmem, vmem],
        out_specs=vmem,
        out_shape=jax.ShapeDtypeStruct((total, width), jnp.bfloat16),
        scratch_shapes=[
            pltpu.VMEM((ny, rows, width), jnp.float32),
            pltpu.VMEM((ny, rows, width), jnp.float32),
            pltpu.VMEM((ny - 1, rows, width), jnp.float32),
            pltpu.VMEM((rows, width), jnp.bfloat16),
            pltpu.VMEM((nz - 1, rows, width), jnp.bfloat16),
            pairs, pairs, across, across, planes, planes, across, across, pairs, pairs,
        ],
        compiler_params=pltpu.CompilerParams(
            collective_id=collective_id, has_side_effects=True, vmem_limit_bytes=16 * 2**20
        ),
        cost_estimate=pl.CostEstimate(
            flops=0, bytes_accessed=40 * 2**20, transcendentals=0
        ),
    )(low, keep)


def direct_act_kernel(
    nt, nz, low_ref, keep_ref, act_ref, near, mine, far, s1, r1, s2, r2, s3, r3
):
    t, z = lax.axis_index("tensor"), lax.axis_index("replica")
    rows, width = mine.shape
    barrier = pltpu.get_barrier_semaphore()
    for d in range(1, nt):
        pl.semaphore_signal(barrier, inc=1, device_id={"tensor": lax.rem(t + d, nt)})
    for d in range(1, nz):
        pl.semaphore_signal(barrier, inc=1, device_id={"replica": lax.rem(z + d, nz)})
    pl.semaphore_wait(barrier, nt + nz - 2)

    def block(index):
        return pl.ds(pl.multiple_of(index * rows, rows), rows)

    copies = []
    for d in range(1, nt):
        peer = lax.rem(t + d, nt)
        copies.append(
            pltpu.make_async_remote_copy(
                low_ref.at[block(peer)], near.at[d - 1], s1.at[d - 1], r1.at[d - 1],
                device_id={"tensor": peer},
            )
        )
        copies[-1].start()
    total = low_ref[block(t), :]
    for d in range(1, nt):
        copies[d - 1].wait()
        total = total + near[d - 1]
    keep = keep_ref[block(t), :]
    own = (total * jnp.concatenate([keep] * (width // keep.shape[1]), axis=1)).astype(jnp.bfloat16)
    mine[...] = own

    copies = []
    for d in range(1, nz):
        peer = lax.rem(z + d, nz)
        copies.append(
            pltpu.make_async_remote_copy(
                mine, far.at[d - 1], s2.at[d - 1], r2.at[d - 1], device_id={"replica": peer}
            )
        )
        copies[-1].start()
    total = own.astype(jnp.float32)
    for d in range(1, nz):
        copies[d - 1].wait()
        total = total + far[d - 1].astype(jnp.float32)
    act_ref[block(t), :] = total.astype(jnp.bfloat16)

    copies = []
    for d in range(1, nt):
        peer = lax.rem(t + d, nt)
        copies.append(
            pltpu.make_async_remote_copy(
                act_ref.at[block(t)], act_ref.at[block(t)], s3.at[d - 1], r3.at[d - 1],
                device_id={"tensor": peer},
            )
        )
        copies[-1].start()
    for copy in copies:
        copy.wait()


def direct_rank_rows(low, keep, nt, nz, collective_id):
    total, width = low.shape
    rows = total // nt
    vmem = pl.BlockSpec(memory_space=pltpu.VMEM)
    near, far = pltpu.SemaphoreType.DMA((nt - 1,)), pltpu.SemaphoreType.DMA((nz - 1,))
    return pl.pallas_call(
        functools.partial(direct_act_kernel, nt, nz),
        in_specs=[vmem, vmem],
        out_specs=vmem,
        out_shape=jax.ShapeDtypeStruct((total, width), jnp.bfloat16),
        scratch_shapes=[
            pltpu.VMEM((nt - 1, rows, width), jnp.float32),
            pltpu.VMEM((rows, width), jnp.bfloat16),
            pltpu.VMEM((nz - 1, rows, width), jnp.bfloat16),
            near, near, far, far, near, near,
        ],
        compiler_params=pltpu.CompilerParams(
            collective_id=collective_id, has_side_effects=True, vmem_limit_bytes=16 * 2**20
        ),
        cost_estimate=pl.CostEstimate(
            flops=0, bytes_accessed=40 * 2**20, transcendentals=0
        ),
    )(low, keep)


def part_kernel(first_ref, adapter_ref, x_ref, rank_ref, w_ref, up_ref, out_ref, spread_ref):
    @pl.when(pl.program_id(0) == 0)
    def _():
        rank_width = rank_ref.shape[1]
        rows, wide = spread_ref.shape
        row = lax.broadcasted_iota(jnp.int32, (rank_width, wide), 0)
        column = lax.broadcasted_iota(jnp.int32, (rank_width, wide), 1)
        repeat = jnp.where(column % rank_width == row, 1.0, 0.0).astype(jnp.bfloat16)
        tiled = jnp.dot(rank_ref[...], repeat, preferred_element_type=jnp.float32)
        owner = first_ref[0] + lax.broadcasted_iota(jnp.int32, (rows, wide), 1) // rank_width
        spread_ref[...] = jnp.where(adapter_ref[...] == owner, tiled, 0.0).astype(jnp.bfloat16)

    out_ref[...] = (
        jnp.dot(x_ref[...], w_ref[...], preferred_element_type=jnp.float32)
        + jnp.dot(spread_ref[...], up_ref[...], preferred_element_type=jnp.float32)
    ).astype(jnp.bfloat16)


def part_rows(x, w, ranks, up, adapter, first, chunk=0, chunks=1):
    rows, depth = x.shape
    columns = w.shape[1] // chunks
    count, rank_width, _ = up.shape
    wide = count * rank_width
    tile = min(512, columns)
    begin = chunk * columns // tile
    return pl.pallas_call(
        part_kernel,
        grid_spec=pltpu.PrefetchScalarGridSpec(
            num_scalar_prefetch=1,
            grid=(columns // tile,),
            in_specs=[
                pl.BlockSpec((rows, 1), lambda n, s: (0, 0)),
                pl.BlockSpec((rows, depth), lambda n, s: (0, 0)),
                pl.BlockSpec((rows, rank_width), lambda n, s: (0, 0)),
                pl.BlockSpec((depth, tile), lambda n, s: (0, begin + n)),
                pl.BlockSpec((wide, tile), lambda n, s: (0, begin + n)),
            ],
            out_specs=pl.BlockSpec((rows, tile), lambda n, s: (0, n)),
            scratch_shapes=[pltpu.VMEM((rows, wide), jnp.bfloat16)],
        ),
        out_shape=jax.ShapeDtypeStruct((rows, columns), jnp.bfloat16),
        compiler_params=pltpu.CompilerParams(vmem_limit_bytes=56 * 2**20),
        cost_estimate=pl.CostEstimate(
            flops=2 * rows * (depth + wide) * columns,
            bytes_accessed=2 * (rows * depth + (depth + wide) * columns + rows * columns),
            transcendentals=0,
        ),
    )(first, adapter, x, ranks, w, up.reshape(wide, up.shape[2]))


def token_tables(seg_lengths, seg_adapter, adapter_rank, total, rank_width):
    seg_ends = jnp.cumsum(seg_lengths)
    positions = jnp.arange(total, dtype=jnp.int32)
    seg_index = jnp.sum((positions[:, None] >= seg_ends[None, :]).astype(jnp.int32), axis=1)
    seg_hot = seg_index[:, None] == jnp.arange(seg_lengths.shape[0], dtype=jnp.int32)[None, :]
    adapter = jnp.sum(jnp.where(seg_hot, seg_adapter[None, :], 0), axis=1)
    adapter_hot = adapter[:, None] == jnp.arange(adapter_rank.shape[0], dtype=jnp.int32)[None, :]
    rank = jnp.sum(jnp.where(adapter_hot, adapter_rank[None, :], 0), axis=1)
    columns = jnp.arange(rank_width, dtype=jnp.int32)
    keep = jnp.where(
        columns[None, :] < rank[:, None], 0.5 * rank_width / rank.astype(jnp.float32)[:, None], 0.0
    )
    return adapter, keep


def reduce_rows(x, nt):
    if nt != 4:
        out = lax.psum_scatter(x, "tensor", scatter_dimension=0, tiled=True)
        return out, out
    t = lax.axis_index("tensor")
    core, y = t % 2, t // 2
    x = x.reshape(2, 2, x.shape[0] // 4, x.shape[1])
    keep = lax.dynamic_index_in_dim(x, core, 1, keepdims=False)
    give = lax.dynamic_index_in_dim(x, 1 - core, 1, keepdims=False)
    got = lax.ppermute(give, "tensor", [(0, 1), (1, 0), (2, 3), (3, 2)])

    def pair(index):
        a = lax.dynamic_index_in_dim(keep, index, 0, keepdims=False)
        b = lax.dynamic_index_in_dim(got, index, 0, keepdims=False)
        return a.astype(jnp.float32) + b.astype(jnp.float32)

    give = pair(1 - y).astype(jnp.bfloat16)
    got2 = lax.ppermute(give, "tensor", [(0, 2), (2, 0), (1, 3), (3, 1)])
    return (pair(y) + got2.astype(jnp.float32)).astype(jnp.bfloat16), give


def shards(nt, nz, h, c, wq, wkv, wo, dqkv, dout, upq, upkv, upo, seg_lengths, seg_adapter, adapter_rank):
    total = h.shape[0] * nz
    depth = h.shape[1]
    r = upq.shape[1]
    sub = nt // nz
    rows = total // nt // PIECES

    def local_piece(x, p):
        return x.reshape(sub, PIECES, rows, depth)[:, p].reshape(sub * rows, depth)

    adapter, keep = token_tables(seg_lengths, seg_adapter, adapter_rank, total, r)
    adapter = adapter.reshape(nt, PIECES, rows)
    keep = keep.reshape(nt, PIECES, rows, r)
    adapters = [adapter[:, p].reshape(nt * rows, 1) for p in range(PIECES)]
    keeps = [keep[:, p].reshape(nt * rows, r) for p in range(PIECES)]
    first_down = (lax.axis_index("replica") * dqkv.shape[0]).astype(jnp.int32)[None]
    first_up = (lax.axis_index("tensor") * upq.shape[0]).astype(jnp.int32)[None]
    table_qkv, table_out = jnp.swapaxes(dqkv, 1, 2), jnp.swapaxes(dout, 1, 2)
    is_value = lax.axis_index("replica") * upkv.shape[2] >= KVD

    gathered = []
    for x, p in [(h, p) for p in range(PIECES)] + [(c, p) for p in range(PIECES)]:
        piece = local_piece(x, p)
        if gathered:
            piece, gathered[-1] = lax.optimization_barrier((piece, gathered[-1]))
        gathered.append(lax.all_gather(piece, "replica", axis=0, tiled=True))

    queries, keyvals, outs = [], [], []
    given, reduced = (), ((), ())
    for piece in range(2 * PIECES):
        p = piece % PIECES
        adapter = adapters[p]
        x = lax.optimization_barrier((gathered[piece], given, reduced[0]))[0]
        if piece < PIECES:
            low = low_rows(x, table_qkv, adapter, first_down)
            act = rank_rows(low, keeps[p], nt, nz, piece)
            rank_kv = jnp.where(is_value, act[:, 2 * r :], act[:, r : 2 * r])
            query = part_rows(x, wq, act[:, :r], upq, adapter, first_up)
            keyval = part_rows(x, wkv, rank_kv, upkv, adapter, first_up)
            query, given_query = reduce_rows(query, nt)
            keyval, given_keyval = reduce_rows(keyval, nt)
            queries.append(query)
            keyvals.append(keyval)
            given, reduced = (given_query, given_keyval), (reduced[1], (query, keyval))
        else:
            low = low_rows(x, table_out, adapter, first_down)
            act = direct_rank_rows(low, keeps[p], nt, nz, piece)
            act = lax.optimization_barrier((act, reduced[1][0]))[0]
            chunks = []
            for chunk in range(OUT_CHUNKS):
                if chunks:
                    act = lax.optimization_barrier((act, chunks[-1][1], reduced[1][1]))[0]
                part = part_rows(x, wo, act, upo, adapter, first_up, chunk, OUT_CHUNKS)
                chunks.append(reduce_rows(part, nt))
            given = tuple(sent for _, sent in chunks)
            outs.append(jnp.concatenate([out for out, _ in chunks], axis=1))
            reduced = (reduced[1], (outs[-1],))
    return tuple(jnp.concatenate(pieces, axis=0) for pieces in (queries, keyvals, outs))


def solution(mesh):
    in_specs = (
        P(("groups", "replica"), "tensor"),
        P(("groups", "replica"), "tensor"),
        P("tensor", "replica"),
        P("tensor", "replica"),
        P("tensor", "replica"),
        P(("groups", "replica"), "tensor", None),
        P(("groups", "replica"), "tensor", None),
        P(("groups", "tensor"), None, "replica"),
        P(("groups", "tensor"), None, "replica"),
        P(("groups", "tensor"), None, "replica"),
        P("groups"),
        P("groups"),
        P("groups"),
    )
    out_specs = (P(("groups", "tensor"), "replica"),) * 3
    body = functools.partial(shards, mesh.shape["tensor"], mesh.shape["replica"])
    return jax.shard_map(body, mesh=mesh, in_specs=in_specs, out_specs=out_specs, check_vma=False)
```
